1024 devices in a mesh: dp: 64 (over y, z_lo), fsdp: 16 (over z_hi, x, core).
Axes of the slice: x: 4, y: 8, z: 16 (z_hi: 2, z_lo: 8; z = z_hi * 8 + z_lo), core: 2. Of those that a mesh axis runs over, the one named last changes fastest.
Arguments:
- expert_weights: bfloat16 [16, 896, 896], P(None, 'fsdp'), may hold values from -0.1875 to 0.1875
- coefficients: float32 [1024, 16], replicated, may hold values from 0.05 to 1
- edge_inputs: bfloat16 [1024, 512, 896], P(('dp', 'fsdp')), may hold values from -6 to 6
- node_cotangent: bfloat16 [1024, 128, 896], P(('dp', 'fsdp')), may hold values from -6 to 6
- rotations: float32 [1024, 7, 7, 512], P(('dp', 'fsdp')), may hold values from -2 to 2
- targets: int32 [1024, 512], P(('dp', 'fsdp')), may hold values from 0 to 127
- counts: int32 [1024], P(('dp', 'fsdp')), may hold values from 128 to 512, as said below
Outputs:
- edge_grads: bfloat16 [1024, 512, 896], P(('dp', 'fsdp'))
- expert_grads: float32 [16, 896, 896], P(None, 'fsdp', 'dp')
The draws below stay inside these ranges and needn't reach their ends.
Inputs may be any that keep to these rules, and one draw needn't show every extreme that they name: `counts`: a multiple of 128; some system has 512 live edges and some has 128.
All inputs are finite; a program needn't handle non-finite values.
Results may differ from the reference program's by a relative error of at most 0.0058.
Values may be sent and summed in bfloat16 or wider, within the bound.
A program may use at most 64 MiB of HBM per device.

```python
import math
import jax
import jax.numpy as jnp
from jax import lax

C = 128
L0 = 7
EXPERTS = 16
EDGE_DEV = 512
BLOCK = 128
ATOMS = 128
K = 896
SYSTEMS = 1024


def draw_counts(key, part):
    key = jax.random.fold_in(key, 11)
    blocks = jax.random.randint(key, (SYSTEMS,), 1, EDGE_DEV // BLOCK + 1)
    counts = (blocks * BLOCK).astype(jnp.int32)
    counts = counts.at[0].set(EDGE_DEV)
    counts = counts.at[1].set(BLOCK)
    return counts


def touch_ends(values, rng, low, high):
    extent = values.shape
    place = [jax.random.randint(jax.random.fold_in(rng, axis), (), 0, extent[axis]) for axis in range(len(extent))]
    values = values.at[tuple(place)].set(low)
    longest = extent.index(max(extent))
    place[longest] = (place[longest] + 1) % extent[longest]
    return values.at[tuple(place)].set(high)


def levels(key, dims, pieces, least, high):
    def one(axis_at, shards_of):
        draws = jax.random.uniform(jax.random.fold_in(jax.random.fold_in(key, 6), axis_at), (shards_of,), jnp.float32, least / len(pieces), high / len(pieces))
        return jnp.repeat(jnp.exp(draws), dims[axis_at] // shards_of).reshape((-1,) + (1,) * (len(dims) - axis_at - 1))

    loudness = one(*pieces[0])
    for cut in pieces[1:]:
        loudness = loudness * one(*cut)
    return loudness


def scatter_about(stream_key, dims, width, bound, pieces=(), kind=jnp.bfloat16):
    values = jax.random.normal(stream_key, dims, jnp.float32) * width
    if len(pieces) > 0:
        values = levels(stream_key, dims, pieces, -0.22, 0.18) * values
    return jnp.clip(values, min=-bound, max=bound).astype(kind)


def setup_inputs(seed: int = 0) -> dict:
    seeds = jax.random.split(jax.random.key(seed), 8)
    return {
        "expert_weights": scatter_about(seeds[0], (EXPERTS, K, K), K ** -0.5, 0.1875, ((1, 16),)),
        "coefficients": jnp.clip(jnp.exp(jax.random.uniform(seeds[1], (SYSTEMS, EXPERTS), jnp.float32, math.log(0.05), math.log(1.0))), 0.05, 1.0),
        "edge_inputs": scatter_about(seeds[2], (SYSTEMS, EDGE_DEV, K), 1.0, 6.0, ((0, 1024),)),
        "node_cotangent": scatter_about(seeds[3], (SYSTEMS, ATOMS, K), 1.0, 6.0, ((0, 1024),)),
        "rotations": scatter_about(seeds[4], (SYSTEMS, L0, L0, EDGE_DEV), 0.4, 2.0, ((0, 1024),), jnp.float32),
        "targets": touch_ends(jax.random.randint(seeds[5], (SYSTEMS, EDGE_DEV), 0, ATOMS), jax.random.fold_in(seeds[5], 1), 0, ATOMS - 1).astype(jnp.int32),
        "counts": draw_counts(jax.random.fold_in(seeds[7], 71), 0),
    }


def reference(expert_weights, coefficients, edge_inputs, node_cotangent, rotations, targets, counts):
    wide = expert_weights.astype(jnp.float32).reshape(EXPERTS, K * K)
    slots = jnp.arange(EDGE_DEV, dtype=jnp.int32)

    def one_system(total, items):
        coef, inputs, nodes, rotation, target, count = items
        merged = jnp.dot(coef[None, :], wide, precision=lax.Precision.HIGHEST).reshape(K, K).astype(jnp.bfloat16)
        picked = nodes[target].reshape(EDGE_DEV, L0, C).astype(jnp.float32)
        turned = jnp.einsum("abi,ibc->iac", rotation, picked, precision=lax.Precision.HIGHEST)
        live = (slots < count).astype(jnp.float32)
        rotated = (turned * live[:, None, None]).reshape(EDGE_DEV, K).astype(jnp.bfloat16)
        grads = lax.dot_general(rotated, merged, (((1,), (1,)), ((), ())), preferred_element_type=jnp.float32)
        weight_grad = lax.dot_general(inputs, rotated, (((0,), (0,)), ((), ())), preferred_element_type=jnp.float32)
        weight_grad = weight_grad.astype(jnp.bfloat16).astype(jnp.float32)
        total = total + coef[:, None, None] * weight_grad[None, :, :]
        return total, grads.astype(jnp.bfloat16)

    start = jnp.zeros((EXPERTS, K, K), jnp.float32)
    total, edge_grads = lax.scan(one_system, start, (coefficients, edge_inputs, node_cotangent, rotations, targets, counts))
    return edge_grads, total
```

```python
import jax
import jax.numpy as jnp
from jax import lax
from jax.experimental import pallas as pl
from jax.experimental.pallas import tpu as pltpu
from jax.sharding import PartitionSpec as P

MESH = pl.DeviceIdType.MESH
F32, BF16 = jnp.float32, jnp.bfloat16
L0, CH, EDGES, ATOMS, K, EXPERTS = 7, 128, 512, 128, 896, 16
NX, NY, NZ, NZL = 4, 8, 16, 8
GROUP = 8
ROWS, COLS = 56, 14
QS = 4
HALF = COLS // 2


def onehot(shape, test):
    rows = lax.broadcasted_iota(jnp.int32, shape, 0)
    cols = lax.broadcasted_iota(jnp.int32, shape, 1)
    return jnp.where(test(rows, cols), 1.0, 0.0).astype(BF16)


def dot(a, b):
    return jnp.dot(a, b, preferred_element_type=F32)


def kernel(
    w_ref, coef_ref, ct_ref, in_ref, node_ref, rot_ref, tgt_ref, cnt_ref,
    eg_ref, xg_ref,
    picked, rot_t, rot_n, in_pad, mix, gs, gr, area, part, zs, zr, total, ys, yr,
    wo, ms, mr, mg,
    g_send, g_recv, g_self, z_send, z_recv, y_send, y_recv,
    w_send, w_recv, a_send, a_recv, m_send, m_recv, m_self,
):
    dp, fs = lax.axis_index("dp"), lax.axis_index("fsdp")
    y, zl = dp // NZL, dp % NZL
    zh, g = fs // GROUP, fs % GROUP
    z = zh * NZL + zl
    py, yq = y % 2, y // 2

    def at(g_to, y_to, z_to):
        return (y_to * NZL + z_to % NZL, (z_to // NZL) * GROUP + g_to)

    near = y + 1 - 2 * py
    far = (y + 7 + 2 * py) % NY
    mirror = NZ - 1 - z
    up, down = (z + 1) % NZ, (z + NZ - 1) % NZ

    def send(src, dst, ssem, rsem, to):
        return pltpu.make_async_remote_copy(
            src_ref=src, dst_ref=dst, send_sem=ssem, recv_sem=rsem, device_id=to, device_id_type=MESH
        )

    barrier = pltpu.get_barrier_semaphore()
    greeted = [at((g + k) % GROUP, y, z) for k in range(1, GROUP)]
    greeted += [at((g + k) % GROUP, near, z) for k in range(GROUP)]
    greeted += [at((g + k) % GROUP, far, z) for k in range(GROUP)]
    greeted += [at(g, y, mirror), at(g, y, up), at(g, y, down)]
    greeted += [at(g, (y + 2 * k) % NY, z) for k in range(1, QS)]
    for to in greeted:
        pl.semaphore_signal(barrier, inc=1, device_id=to, device_id_type=MESH)

    hot = jnp.where(
        lax.broadcasted_iota(jnp.int32, (ATOMS, EDGES), 0) == tgt_ref[...], 1.0, 0.0
    ).astype(BF16)
    for b in range(L0):
        picked[b * CH : (b + 1) * CH, :] = lax.dot_general(
            node_ref[:, b * CH : (b + 1) * CH], hot, (((0,), (0,)), ((), ())), preferred_element_type=F32
        )
    live = jnp.where(
        lax.broadcasted_iota(jnp.int32, (1, EDGES), 1) < cnt_ref[0], 1.0, 0.0
    )

    def turn(i, _):
        start = pl.multiple_of(i * 16, 16)
        for lo in range(0, EDGES, 256):
            lanes = slice(lo, lo + 256)
            cols = [picked[pl.ds(b * CH + start, 16), lanes] for b in range(L0)]
            for a in range(L0):
                acc = rot_ref[a, 0:1, lanes] * cols[0]
                for b in range(1, L0):
                    acc += rot_ref[a, b : b + 1, lanes] * cols[b]
                rot_t[pl.ds(a * CH + start, 16), lanes] = (acc * live[:, lanes]).astype(BF16)
        return 0

    lax.fori_loop(0, CH // 16, turn, 0)

    for h in range(GROUP):
        put = onehot(
            (K, 128),
            lambda r, l, h=h: (r == (l // 64) * (K // 2) + h * ROWS + l % 64) & (l % 64 < ROWS),
        )
        in_pad[:, h * 128 : (h + 1) * 128] = dot(in_ref[...], put).astype(BF16)

    spread = onehot((256, 16), lambda m, e: m % 16 == e)
    gather = onehot((16, 256), lambda s, k: k // 16 == s)
    same = onehot((256, 256), lambda m, k: m // 16 == k % 16).astype(F32)
    for pair in range(2):
        coef = ct_ref[pair]
        high = coef.astype(BF16)
        low = (coef - high.astype(F32)).astype(BF16)
        for n, piece in enumerate((high, low)):
            wide = dot(dot(spread, piece).astype(BF16), gather)
            mix[pair, n] = (wide * same).astype(BF16)

    pl.semaphore_wait(barrier, len(greeted))

    w_copy = send(w_ref.at[y], wo.at[y], w_send.at[0], w_recv.at[0], at(g, y, mirror))
    w_copy.start()

    def g_copies(q, other):
        out = []
        for k in range(GROUP):
            g_to = (g + k) % GROUP
            if k > 0:
                out.append(send(
                    gs.at[q, py, g_to], gr.at[q, g], g_send.at[q, k], g_recv.at[q, k], at(g_to, y, z)
                ))
            out.append(send(
                gs.at[q, 1 - py, g_to], gr.at[q, GROUP + g],
                g_send.at[q, GROUP + k], g_recv.at[q, GROUP + k], at(g_to, other, z),
            ))
        return out

    def g_own(q):
        return pltpu.make_async_copy(gs.at[q, py, g], gr.at[q, g], g_self.at[q])

    def grad_chunk(q, other):
        for p in range(2):
            rows = rot_t[(2 * q + p) * 112 : (2 * q + p + 1) * 112, :]
            for h in range(0, GROUP, 2):
                block = dot(rows, in_pad[:, h * 128 : (h + 2) * 128]).astype(BF16)
                gs[q, p, h] = block[:, :128]
                gs[q, p, h + 1] = block[:, 128:]
        g_own(q).start()
        for copy in g_copies(q, other):
            copy.start()

    others = [near, near, far, far]
    for q in range(QS):
        grad_chunk(q, others[q])
    rot_n[...] = rot_t[...].T

    low_lanes = lax.broadcasted_iota(jnp.int32, (16, 128), 1) < 64

    def swap(v):
        return pltpu.roll(v, 64, 1)

    def contract(q):
        g_own(q).wait()
        for copy in g_copies(q, others[q]):
            copy.wait_recv()
        for t in range(7):
            block = gr[q, :, t * 16 : (t + 1) * 16, :].reshape(256, 128)
            made = dot(mix[q // 2, 0], block) + dot(mix[q // 2, 1], block)
            area[t * 16 : (t + 1) * 16] = made.reshape(16, 16, 128)

        def pack(i, _):
            for k in range(HALF):
                first, second = area[i * COLS + k], area[i * COLS + HALF + k]
                part[q, i, k] = jnp.where(low_lanes, first, swap(second))
                part[q, NZL + i, k] = jnp.where(low_lanes, swap(first), second)
            return 0

        lax.fori_loop(0, NZL, pack, 0)

    def steps(q, way):
        return 8 if way == q % 2 else 7

    def z_copy(q, way, s):
        return send(
            zs.at[q, way, s], zr.at[q, way, s], z_send.at[q, way, s], z_recv.at[q, way, s],
            at(g, y, up if way == 0 else down),
        )

    def ring_step(q, s):
        for way in range(2):
            n = steps(q, way)
            if s >= n:
                continue
            ahead = n - s
            owner = (z + ahead) % NZ if way == 0 else (z + NZ - ahead) % NZ
            value = part[q, owner]
            if s > 0:
                z_copy(q, way, s - 1).wait_recv()
                value += zr[q, way, s - 1].astype(F32)
            zs[q, way, s] = value.astype(BF16)
            z_copy(q, way, s).start()

    def ring_end(q):
        value = part[q, z]
        for way in range(2):
            n = steps(q, way)
            z_copy(q, way, n - 1).wait_recv()
            value += zr[q, way, n - 1].astype(F32)
        total[q] = value

    def m_copies(side):
        slot = (zh if side == 0 else 1 - zh) * GROUP + g
        return [
            send(
                ms.at[side, (g + k) % GROUP], mr.at[slot], m_send.at[side, k], m_recv.at[side, k],
                at((g + k) % GROUP, y, z),
            )
            for k in range(1, GROUP)
        ]

    def m_own(side):
        slot = (zh if side == 0 else 1 - zh) * GROUP + g
        return pltpu.make_async_copy(ms.at[side, g], mr.at[slot], m_self.at[side])

    def merge(side, source):
        tail = jnp.zeros((8, 128), F32)

        def block(i, _):
            lanes = pl.ds(pl.multiple_of(i * 128, 128), 128)
            for first in range(0, GROUP, 4):
                sums = [jnp.zeros((ROWS, 128), F32) for _ in range(4)]
                for e in range(0, EXPERTS, 2):
                    both = source[e // 2, :, lanes].astype(F32)
                    for j in range(4):
                        sums[j] += coef_ref[first + j, e] * both[:ROWS]
                        sums[j] += coef_ref[first + j, e + 1] * both[ROWS:]
                for j in range(4):
                    ms[side, first + j, :, lanes] = jnp.concatenate([sums[j], tail], 0).astype(BF16)
            return 0

        lax.fori_loop(0, K // 128, block, 0)
        m_own(side).start()
        for copy in m_copies(side):
            copy.start()

    def a_copy(way, s):
        piece = (y + NY - s) % NY if way == 0 else (y + s) % NY
        to = (y + 1) % NY if way == 0 else (y + NY - 1) % NY
        return send(wo.at[piece], wo.at[piece], a_send.at[way, s], a_recv.at[way, s], at(g, to, z))

    def a_came(way, s):
        piece = (y + NY - s - 1) % NY if way == 0 else (y + s + 1) % NY
        return send(wo.at[piece], wo.at[piece], a_send.at[way, s], a_recv.at[way, s], at(g, y, mirror))

    def gather_step(s):
        for way in range(2):
            if s >= 4 - way:
                continue
            if s > 0:
                a_came(way, s - 1).wait_recv()
            a_copy(way, s).start()

    done = [0] * QS

    def advance(q, count=1):
        for _ in range(count):
            if done[q] < 8:
                ring_step(q, done[q])
                done[q] += 1

    for q in range(QS):
        contract(q)
        advance(q)
        for before in range(q):
            advance(before, 2)
    merge(0, w_ref)
    w_copy.wait_recv()
    gather_step(0)
    for wave in range(7):
        for q in range(QS):
            advance(q)
        if wave in (1, 3, 5):
            gather_step(wave // 2 + 1)
    for q in range(QS):
        ring_end(q)

    def y_copy(k):
        q = (yq + k) % QS
        return send(ys.at[k], yr.at[k], y_send.at[k], y_recv.at[k], at(g, 2 * q + py, z))

    for k in range(1, QS):
        ys[k] = total[(yq + k) % QS].astype(BF16)
        y_copy(k).start()

    a_came(1, 2).wait_recv()
    a_came(0, 3).wait_recv()
    merge(1, wo)

    value = total[yq]
    for k in range(1, QS):
        y_copy(k).wait_recv()
        value += yr[k].astype(F32)
    for k in range(HALF):
        xg_ref[k] = value[k]
        xg_ref[HALF + k] = swap(value[k])

    for side in range(2):
        m_own(side).wait()
        for copy in m_copies(side):
            copy.wait_recv()
    for lo in range(0, K, 128):
        blocks = [mr[f, :, lo : lo + 128].astype(F32)[:ROWS] for f in range(2 * GROUP)]
        mg[:, lo : lo + 128] = jnp.concatenate(blocks, 0).astype(BF16)
    for lo in range(0, EDGES, 128):
        eg_ref[lo : lo + 128, :] = lax.dot_general(
            rot_n[lo : lo + 128, :], mg[...], (((1,), (1,)), ((), ())), preferred_element_type=F32
        ).astype(BF16)

    w_copy.wait_send()
    for q in range(QS):
        for copy in g_copies(q, others[q]):
            copy.wait_send()
        for way in range(2):
            for s in range(steps(q, way)):
                z_copy(q, way, s).wait_send()
    for k in range(1, QS):
        y_copy(k).wait_send()
    for way in range(2):
        for s in range(4 - way):
            a_copy(way, s).wait_send()
    for side in range(2):
        for copy in m_copies(side):
            copy.wait_send()


def per_device(
    expert_weights, coefficients, edge_inputs, node_cotangent, rotations, targets, counts
):
    dp, fs = lax.axis_index("dp"), lax.axis_index("fsdp")
    y, zl, zh = dp // NZL, dp % NZL, fs // GROUP

    def of_group(y_of):
        start = (y_of * NZL + zl) * (2 * GROUP) + zh * GROUP
        return lax.dynamic_slice_in_dim(coefficients, start, GROUP, 0)

    py = y % 2
    own = of_group(y)
    pairs = jnp.stack([
        jnp.concatenate([own, of_group(y + 1 - 2 * py)], 0).T,
        jnp.concatenate([own, of_group((y + 7 + 2 * py) % NY)], 0).T,
    ])
    vmem, smem = pl.BlockSpec(memory_space=pltpu.VMEM), pl.BlockSpec(memory_space=pltpu.SMEM)
    dma, shape = pltpu.SemaphoreType.DMA, pltpu.VMEM
    edge_grads, grads = pl.pallas_call(
        kernel,
        out_shape=(
            jax.ShapeDtypeStruct((EDGES, K), BF16),
            jax.ShapeDtypeStruct((COLS, EXPERTS, 128), F32),
        ),
        in_specs=[vmem, smem, vmem, vmem, vmem, vmem, vmem, smem],
        out_specs=(vmem, vmem),
        scratch_shapes=[
            shape((K, EDGES), F32),
            shape((K, EDGES), BF16),
            shape((EDGES, K), BF16),
            shape((EDGES, GROUP * 128), BF16),
            shape((2, 2, 256, 256), BF16),
            shape((QS, 2, GROUP, 112, 128), BF16),
            shape((QS, 2 * GROUP, 112, 128), BF16),
            shape((112, EXPERTS, 128), F32),
            shape((QS, NZ, HALF, EXPERTS, 128), F32),
            shape((QS, 2, 8, HALF, EXPERTS, 128), BF16),
            shape((QS, 2, 8, HALF, EXPERTS, 128), BF16),
            shape((QS, HALF, EXPERTS, 128), F32),
            shape((QS, HALF, EXPERTS, 128), BF16),
            shape((QS, HALF, EXPERTS, 128), BF16),
            shape((NY, 112, K), BF16),
            shape((2, GROUP, 64, K), BF16),
            shape((2 * GROUP, 64, K), BF16),
            shape((K, K), BF16),
            dma((QS, 16)), dma((QS, 16)), dma((QS,)),
            dma((QS, 2, 8)), dma((QS, 2, 8)),
            dma((QS,)), dma((QS,)),
            dma((1,)), dma((1,)),
            dma((2, 4)), dma((2, 4)),
            dma((2, GROUP)), dma((2, GROUP)), dma((2,)),
        ],
        compiler_params=pltpu.CompilerParams(
            collective_id=0, has_side_effects=True, vmem_limit_bytes=48 * 1024 * 1024
        ),
        name="edge_block_backward",
    )(
        expert_weights.reshape(NY, 112, K),
        own,
        pairs,
        edge_inputs[0],
        node_cotangent[0],
        rotations[0],
        targets,
        counts,
    )
    return edge_grads[None], jnp.transpose(grads[:, :, :ROWS], (1, 2, 0))


def solution(mesh):
    placed = (
        P(None, "fsdp", None),
        P(),
        P(("dp", "fsdp"), None, None),
        P(("dp", "fsdp"), None, None),
        P(("dp", "fsdp"), None, None, None),
        P(("dp", "fsdp"), None),
        P(("dp", "fsdp")),
    )
    return jax.shard_map(
        per_device,
        mesh=mesh,
        in_specs=placed,
        out_specs=(P(("dp", "fsdp"), None, None), P(None, "fsdp", "dp")),
        check_vma=False,
    )
```

```python
import jax
import jax.numpy as jnp
from jax import lax
from jax.experimental import pallas as pl
from jax.experimental.pallas import tpu as pltpu
from jax.sharding import PartitionSpec as P

MESH = pl.DeviceIdType.MESH
F32, BF16 = jnp.float32, jnp.bfloat16
L0, CH, EDGES, ATOMS, K, EXPERTS = 7, 128, 512, 128, 896, 16
NX, NY, NZ, NZL = 4, 8, 16, 8
GROUP = 8
ROWS, COLS = 56, 14
QS = 4
HALF = COLS // 2
OWN_AT = 0
FIRST_N = 4
OTHER_AT = ((4, 3), (5, 2), (6, 1), (7, 0), (), (), ())
LANES = K // 128


def onehot(shape, test):
    rows = lax.broadcasted_iota(jnp.int32, shape, 0)
    cols = lax.broadcasted_iota(jnp.int32, shape, 1)
    return jnp.where(test(rows, cols), 1.0, 0.0).astype(BF16)


def dot(a, b):
    return jnp.dot(a, b, preferred_element_type=F32)


def kernel(
    w_hbm, coef_ref, ct_ref, in_hbm, node_hbm, rot_hbm, tgt_ref, cnt_ref,
    eg_ref, xg_ref,
    w_ref, in_ref, node_ref, rot_ref, loads, picked, rot_t, rot_n, in_pad, mix, gs, gr, area, part, zs, zr, total, ys, yr,
    wo, ms, mo, mr, mg,
    g_send, g_recv, g_self, z_send, z_recv, y_send, y_recv,
    w_send, w_recv, o_send, o_recv, m_send, m_recv, m_self,
):
    dp, fs = lax.axis_index("dp"), lax.axis_index("fsdp")
    y, zl = lax.div(dp, NZL), lax.rem(dp, NZL)
    zh, g = lax.div(fs, GROUP), lax.rem(fs, GROUP)
    z = zh * NZL + zl
    py, yq = lax.rem(y, 2), lax.div(y, 2)

    def at(g_to, y_to, z_to):
        return (y_to * NZL + lax.rem(z_to, NZL), lax.div(z_to, NZL) * GROUP + g_to)

    near = y + 1 - 2 * py
    far = lax.rem(y + 7 + 2 * py, NY)
    mirror = NZ - 1 - z
    up, down = lax.rem(z + 1, NZ), lax.rem(z + NZ - 1, NZ)

    def send(src, dst, ssem, rsem, to):
        return pltpu.make_async_remote_copy(
            src_ref=src, dst_ref=dst, send_sem=ssem, recv_sem=rsem, device_id=to, device_id_type=MESH
        )

    load = [
        pltpu.make_async_copy(src, dst, loads.at[n])
        for n, (src, dst) in enumerate(
            ((node_hbm, node_ref), (rot_hbm, rot_ref), (in_hbm, in_ref), (w_hbm, w_ref))
        )
    ]
    for copy in load:
        copy.start()

    barrier = pltpu.get_barrier_semaphore()
    greeted = [
        at(lax.rem(g + k, GROUP), lax.rem(y + n, NY), z)
        for n in range(NY) for k in range(GROUP) if n + k > 0
    ]
    greeted += [at(g, y, mirror), at(g, y, up), at(g, y, down)]
    for to in greeted:
        pl.semaphore_signal(barrier, inc=1, device_id=to, device_id_type=MESH)

    hot = jnp.where(
        lax.broadcasted_iota(jnp.int32, (ATOMS, EDGES), 0) == tgt_ref[...], 1.0, 0.0
    ).astype(BF16)
    load[0].wait()
    for b in range(L0):
        picked[b * CH : (b + 1) * CH, :] = lax.dot_general(
            node_ref[:, b * CH : (b + 1) * CH], hot, (((0,), (0,)), ((), ())), preferred_element_type=F32
        )
    live = jnp.where(
        lax.broadcasted_iota(jnp.int32, (1, EDGES), 1) < cnt_ref[0], 1.0, 0.0
    )

    def turn(degrees):
        def rows(i, _):
            start = pl.multiple_of(i * 16, 16)
            for n in range(EDGES // 128):
                lanes = slice(n * 128, (n + 1) * 128)
                cols = [picked[pl.ds(b * CH + start, 16), lanes] for b in range(L0)]
                for a in degrees:
                    acc = None
                    for b in range(L0):
                        row = (a * L0 + b) * (EDGES // 128) + n
                        term = rot_ref[row : row + 1, :] * cols[b]
                        acc = term if acc is None else acc + term
                    rot_t[pl.ds(a * CH + start, 16), lanes] = (acc * live[:, lanes]).astype(BF16)
            return 0

        lax.fori_loop(0, CH // 16, rows, 0)

    load[1].wait()
    turn((0, 1))

    pl.semaphore_wait(barrier, len(greeted))

    own_lanes = pl.ds(pl.multiple_of(lax.rem(y, LANES) * 128, 128), 128)
    w_copy = send(
        w_hbm.at[:, :, own_lanes], wo, w_send.at[0], w_recv.at[0], at(g, y, mirror)
    )

    @pl.when(y < LANES)
    def _():
        w_copy.start()

    load[2].wait()
    for h in range(GROUP):
        block = None
        for half in range(2):
            first = half * (K // 2) + h * ROWS
            lo = first // 128 * 128
            hi = -(-(first + ROWS) // 128) * 128
            put = onehot(
                (hi - lo, 128),
                lambda r, l, half=half, d=first - lo: (r == d + l - half * 64)
                & (l >= half * 64) & (l < half * 64 + ROWS),
            )
            part_of = dot(in_ref[:, lo:hi], put)
            block = part_of if block is None else block + part_of
        in_pad[:, h * 128 : (h + 1) * 128] = block.astype(BF16)

    def g_copies(q, other):
        out = []
        for k in range(GROUP):
            g_to = lax.rem(g + k, GROUP)
            if k > 0:
                out.append(send(
                    gs.at[q, py, g_to], gr.at[q, g], g_send.at[q, k], g_recv.at[q, k], at(g_to, y, z)
                ))
            out.append(send(
                gs.at[q, 1 - py, g_to], gr.at[q, GROUP + g],
                g_send.at[q, GROUP + k], g_recv.at[q, GROUP + k], at(g_to, other, z),
            ))
        return out

    def g_own(q):
        return pltpu.make_async_copy(gs.at[q, py, g], gr.at[q, g], g_self.at[q])

    def grad_chunk(q, other):
        for p in range(2):
            rows = rot_t[(2 * q + p) * 112 : (2 * q + p + 1) * 112, :]
            for h in range(0, GROUP, 2):
                block = dot(rows, in_pad[:, h * 128 : (h + 2) * 128]).astype(BF16)
                gs[q, p, h] = block[:, :128]
                gs[q, p, h + 1] = block[:, 128:]
        g_own(q).start()
        for copy in g_copies(q, other):
            copy.start()

    others = [near, near, far, far]
    for q in range(QS):
        if q > 0:
            turn(((2, 3), (4, 5), (6,))[q - 1])
        grad_chunk(q, others[q])
    rot_n[...] = rot_t[...].T

    spread = onehot((256, 16), lambda m, e: m % 16 == e)
    gather = onehot((16, 256), lambda s, k: k // 16 == s)
    same = onehot((256, 256), lambda m, k: m // 16 == k % 16).astype(F32)
    for pair in range(2):
        coef = ct_ref[pair]
        high = coef.astype(BF16)
        low = (coef - high.astype(F32)).astype(BF16)
        for n, piece in enumerate((high, low)):
            wide = dot(dot(spread, piece).astype(BF16), gather)
            mix[pair, n] = (wide * same).astype(BF16)

    low_lanes = lax.broadcasted_iota(jnp.int32, (16, 128), 1) < 64

    def swap(v):
        return pltpu.roll(v, 64, 1)

    def contract(q):
        g_own(q).wait()
        for copy in g_copies(q, others[q]):
            copy.wait_recv()
        for t in range(7):
            block = gr[q, :, t * 16 : (t + 1) * 16, :].reshape(256, 128)
            made = dot(mix[q // 2, 0], block) + dot(mix[q // 2, 1], block)
            area[t * 16 : (t + 1) * 16] = made.reshape(16, 16, 128)

        def pack(i, _):
            for k in range(HALF):
                first, second = area[i * COLS + k], area[i * COLS + HALF + k]
                part[q, i, k] = jnp.where(low_lanes, first, swap(second))
                part[q, NZL + i, k] = jnp.where(low_lanes, swap(first), second)
            return 0

        lax.fori_loop(0, NZL, pack, 0)

    def steps(q, way):
        return 8 if way == q % 2 else 7

    def z_copy(q, way, s):
        return send(
            zs.at[q, way, s], zr.at[q, way, s], z_send.at[q, way, s], z_recv.at[q, way, s],
            at(g, y, up if way == 0 else down),
        )

    def ring_step(q, s):
        for way in range(2):
            n = steps(q, way)
            if s >= n:
                continue
            ahead = n - s
            owner = lax.rem(z + ahead, NZ) if way == 0 else lax.rem(z + NZ - ahead, NZ)
            value = part[q, owner]
            if s > 0:
                z_copy(q, way, s - 1).wait_recv()
                value += zr[q, way, s - 1].astype(F32)
            zs[q, way, s] = value.astype(BF16)
            z_copy(q, way, s).start()

    def ring_end(q):
        value = part[q, z]
        for way in range(2):
            n = steps(q, way)
            z_copy(q, way, n - 1).wait_recv()
            value += zr[q, way, n - 1].astype(F32)
        total[q] = value

    def m_copies():
        return [
            send(
                ms.at[lax.rem(g + k, GROUP)], mr.at[zh * GROUP + g], m_send.at[k], m_recv.at[k],
                at(lax.rem(g + k, GROUP), y, z),
            )
            for k in range(1, GROUP)
        ]

    def m_own():
        return pltpu.make_async_copy(ms.at[g], mr.at[zh * GROUP + g], m_self.at[0])

    tail = jnp.zeros((8, 128), F32)

    def mixed(first, source, lanes):
        sums = [None] * 4
        for e in range(0, EXPERTS, 2):
            both = source[e // 2, :, lanes].astype(F32)
            for j in range(4):
                term = coef_ref[first + j, e] * both[:ROWS] + coef_ref[first + j, e + 1] * both[ROWS:]
                sums[j] = term if e == 0 else sums[j] + term
        return [jnp.concatenate([v, tail], 0).astype(BF16) for v in sums]

    def merge_own():
        def block(i, _):
            lanes = pl.ds(pl.multiple_of(i * 128, 128), 128)
            for first in range(0, GROUP, 4):
                for j, v in enumerate(mixed(y * GROUP + first, w_ref, lanes)):
                    ms[first + j, i] = v
            return 0

        load[3].wait()
        lax.fori_loop(0, LANES, block, 0)
        m_own().start()
        for copy in m_copies():
            copy.start()

    def o_copies(n):
        return [
            send(
                mo.at[n, lax.rem(g + k, GROUP)], mr.at[(1 - zh) * GROUP + g, lax.rem(y, LANES)],
                o_send.at[n, k], o_recv.at[n, k], at(lax.rem(g + k, GROUP), lax.rem(y + n, NY), z),
            )
            for k in range(GROUP) if n + k > 0
        ]

    def o_own():
        return pltpu.make_async_copy(
            mo.at[0, g], mr.at[(1 - zh) * GROUP + g, lax.rem(y, LANES)], m_self.at[1]
        )

    def merge_other(n):
        @pl.when(y < LANES)
        def _():
            if n == FIRST_N:
                w_copy.wait_recv()
            for first in range(0, GROUP, 4):
                rows = lax.rem(y + n, NY) * GROUP + first
                for j, v in enumerate(mixed(rows, wo, slice(None))):
                    mo[n, first + j] = v
            if n == 0:
                o_own().start()
            for copy in o_copies(n):
                copy.start()

    def other_came(n):
        @pl.when(lax.rem(y + NY - n, NY) < LANES)
        def _():
            if n == 0:
                o_own().wait()
            for copy in o_copies(n):
                copy.wait_recv()

    def other_left(n):
        @pl.when(y < LANES)
        def _():
            for copy in o_copies(n):
                copy.wait_send()

    done = [0] * QS

    def advance(q, count=1):
        for _ in range(count):
            if done[q] < 8:
                ring_step(q, done[q])
                done[q] += 1

    for q in range(QS):
        if q == OWN_AT:
            merge_own()
        contract(q)
        advance(q)
        if q == 2:
            advance(0)
    for wave in range(7):
        if wave + QS == OWN_AT:
            merge_own()
        for n in OTHER_AT[wave]:
            merge_other(n)
        for q in range(QS):
            advance(q)
    for q in range(QS):
        ring_end(q)

    def y_copy(k):
        q = lax.rem(yq + k, QS)
        return send(ys.at[k], yr.at[k], y_send.at[k], y_recv.at[k], at(g, 2 * q + py, z))

    for k in range(1, QS):
        ys[k] = total[lax.rem(yq + k, QS)].astype(BF16)
        y_copy(k).start()

    m_own().wait()
    for copy in m_copies():
        copy.wait_recv()
    for n in range(NY):
        other_came(n)
    for i in range(LANES):
        blocks = [mr[f, i].astype(F32)[:ROWS] for f in range(2 * GROUP)]
        mg[:, i * 128 : (i + 1) * 128] = jnp.concatenate(blocks, 0).astype(BF16)
    for lo in range(0, EDGES, 128):
        eg_ref[lo : lo + 128, :] = lax.dot_general(
            rot_n[lo : lo + 128, :], mg[...], (((1,), (1,)), ((), ())), preferred_element_type=F32
        ).astype(BF16)

    value = total[yq]
    for k in range(1, QS):
        y_copy(k).wait_recv()
        value += yr[k].astype(F32)
    for k in range(HALF):
        xg_ref[k] = value[k]
        xg_ref[HALF + k] = swap(value[k])


    @pl.when(y < LANES)
    def _():
        w_copy.wait_send()

    for q in range(QS):
        for copy in g_copies(q, others[q]):
            copy.wait_send()
        for way in range(2):
            for s in range(steps(q, way)):
                z_copy(q, way, s).wait_send()
    for k in range(1, QS):
        y_copy(k).wait_send()
    for copy in m_copies():
        copy.wait_send()
    for n in range(NY):
        other_left(n)


def per_device(
    expert_weights, coefficients, edge_inputs, node_cotangent, rotations, targets, counts
):
    dp, fs = lax.axis_index("dp"), lax.axis_index("fsdp")
    y, zl, zh = lax.div(dp, NZL), lax.rem(dp, NZL), lax.div(fs, GROUP)

    grouped = coefficients.reshape(NY, NZL, 2, GROUP, EXPERTS)
    level = lax.dynamic_slice(grouped, (0, zl, zh, 0, 0), (NY, 1, 1, GROUP, EXPERTS))
    level = level.reshape(NY, GROUP, EXPERTS)

    def of_group(y_of):
        return lax.dynamic_slice_in_dim(level, y_of, 1, 0)[0]

    py = lax.rem(y, 2)
    own = of_group(y)
    pairs = jnp.stack([
        jnp.concatenate([own, of_group(y + 1 - 2 * py)], 0).T,
        jnp.concatenate([own, of_group(lax.rem(y + 7 + 2 * py, NY))], 0).T,
    ])
    vmem, smem = pl.BlockSpec(memory_space=pltpu.VMEM), pl.BlockSpec(memory_space=pltpu.SMEM)
    hbm = pl.BlockSpec(memory_space=pltpu.HBM)
    dma, shape = pltpu.SemaphoreType.DMA, pltpu.VMEM
    edge_grads, grads = pl.pallas_call(
        kernel,
        out_shape=(
            jax.ShapeDtypeStruct((EDGES, K), BF16),
            jax.ShapeDtypeStruct((COLS, EXPERTS, 128), F32),
        ),
        in_specs=[hbm, smem, vmem, hbm, hbm, hbm, vmem, smem],
        out_specs=(vmem, vmem),
        scratch_shapes=[
            shape((NY, 112, K), BF16),
            shape((EDGES, K), BF16),
            shape((ATOMS, K), BF16),
            shape((L0 * L0 * EDGES // 128, 128), F32),
            dma((4,)),
            shape((K, EDGES), F32),
            shape((K, EDGES), BF16),
            shape((EDGES, K), BF16),
            shape((EDGES, GROUP * 128), BF16),
            shape((2, 2, 256, 256), BF16),
            shape((QS, 2, GROUP, 112, 128), BF16),
            shape((QS, 2 * GROUP, 112, 128), BF16),
            shape((112, EXPERTS, 128), F32),
            shape((QS, NZ, HALF, EXPERTS, 128), F32),
            shape((QS, 2, 8, HALF, EXPERTS, 128), BF16),
            shape((QS, 2, 8, HALF, EXPERTS, 128), BF16),
            shape((QS, HALF, EXPERTS, 128), F32),
            shape((QS, HALF, EXPERTS, 128), BF16),
            shape((QS, HALF, EXPERTS, 128), BF16),
            shape((NY, 112, 128), BF16),
            shape((GROUP, LANES, 64, 128), BF16),
            shape((NY, GROUP, 64, 128), BF16),
            shape((2 * GROUP, LANES, 64, 128), BF16),
            shape((K, K), BF16),
            dma((QS, 16)), dma((QS, 16)), dma((QS,)),
            dma((QS, 2, 8)), dma((QS, 2, 8)),
            dma((QS,)), dma((QS,)),
            dma((1,)), dma((1,)),
            dma((NY, GROUP)), dma((NY, GROUP)),
            dma((GROUP,)), dma((GROUP,)), dma((2,)),
        ],
        compiler_params=pltpu.CompilerParams(
            collective_id=0, has_side_effects=True, vmem_limit_bytes=48 * 1024 * 1024
        ),
        name="edge_block_backward",
    )(
        expert_weights.reshape(NY, 112, K),
        level.reshape(NY * GROUP, EXPERTS),
        pairs,
        edge_inputs[0],
        node_cotangent[0],
        rotations.reshape(L0 * L0 * EDGES // 128, 128),
        targets,
        counts,
    )
    return edge_grads[None], jnp.transpose(grads[:, :, :ROWS], (1, 2, 0))


def solution(mesh):
    placed = (
        P(None, "fsdp", None),
        P(),
        P(("dp", "fsdp"), None, None),
        P(("dp", "fsdp"), None, None),
        P(("dp", "fsdp"), None, None, None),
        P(("dp", "fsdp"), None),
        P(("dp", "fsdp")),
    )
    return jax.shard_map(
        per_device,
        mesh=mesh,
        in_specs=placed,
        out_specs=(P(("dp", "fsdp"), None, None), P(None, "fsdp", "dp")),
        check_vma=False,
    )
```

```python
import jax
import jax.numpy as jnp
from jax import lax
from jax.experimental import pallas as pl
from jax.experimental.pallas import tpu as pltpu
from jax.sharding import PartitionSpec as P

MESH = pl.DeviceIdType.MESH
F32, BF16 = jnp.float32, jnp.bfloat16
L0, CH, EDGES, ATOMS, K, EXPERTS = 7, 128, 512, 128, 896, 16
NX, NY, NZ, NZL = 4, 8, 16, 8
GROUP = 8
ROWS, COLS = 56, 14
QS = 4
HALF = COLS // 2
OWN_AT = 0
FIRST_N = 4
OTHER_AT = ((4, 3), (5, 2), (6, 1), (7, 0), (), (), ())
LANES = K // 128


def onehot(shape, test):
    rows = lax.broadcasted_iota(jnp.int32, shape, 0)
    cols = lax.broadcasted_iota(jnp.int32, shape, 1)
    return jnp.where(test(rows, cols), 1.0, 0.0).astype(BF16)


def dot(a, b):
    return jnp.dot(a, b, preferred_element_type=F32)


def kernel(
    w_hbm, coef_ref, ct_ref, in_hbm, node_hbm, rot_hbm, tgt_ref, cnt_ref,
    eg_ref, xg_ref,
    w_ref, in_ref, node_ref, rot_ref, loads, picked, rot_t, rot_n, in_pad, mix, gs, gr, area, part, zs, zr, total, ys, yr,
    wo, ms, mo, mr, mg,
    g_send, g_recv, g_self, z_send, z_recv, y_send, y_recv,
    w_send, w_recv, o_send, o_recv, m_send, m_recv, m_self,
):
    dp, fs = lax.axis_index("dp"), lax.axis_index("fsdp")
    y, zl = lax.div(dp, NZL), lax.rem(dp, NZL)
    zh, g = lax.div(fs, GROUP), lax.rem(fs, GROUP)
    z = zh * NZL + zl
    py, yq = lax.rem(y, 2), lax.div(y, 2)

    def at(g_to, y_to, z_to):
        return (y_to * NZL + lax.rem(z_to, NZL), lax.div(z_to, NZL) * GROUP + g_to)

    near = y + 1 - 2 * py
    far = lax.rem(y + 7 + 2 * py, NY)
    mirror = NZ - 1 - z
    up, down = lax.rem(z + 1, NZ), lax.rem(z + NZ - 1, NZ)

    def send(src, dst, ssem, rsem, to):
        return pltpu.make_async_remote_copy(
            src_ref=src, dst_ref=dst, send_sem=ssem, recv_sem=rsem, device_id=to, device_id_type=MESH
        )

    load = [
        pltpu.make_async_copy(src, dst, loads.at[n])
        for n, (src, dst) in enumerate(
            ((node_hbm, node_ref), (rot_hbm, rot_ref), (in_hbm, in_ref), (w_hbm, w_ref))
        )
    ]
    for copy in load:
        copy.start()

    barrier = pltpu.get_barrier_semaphore()
    greeted = [
        at(lax.rem(g + k, GROUP), lax.rem(y + n, NY), z)
        for n in range(NY) for k in range(GROUP) if n + k > 0
    ]
    greeted += [at(g, y, mirror), at(g, y, up), at(g, y, down)]
    for to in greeted:
        pl.semaphore_signal(barrier, inc=1, device_id=to, device_id_type=MESH)

    hot = jnp.where(
        lax.broadcasted_iota(jnp.int32, (ATOMS, EDGES), 0) == tgt_ref[...], 1.0, 0.0
    ).astype(BF16)
    load[0].wait()
    for b in range(L0):
        picked[b * CH : (b + 1) * CH, :] = lax.dot_general(
            node_ref[:, b * CH : (b + 1) * CH], hot, (((0,), (0,)), ((), ())), preferred_element_type=F32
        )
    live = jnp.where(
        lax.broadcasted_iota(jnp.int32, (1, EDGES), 1) < cnt_ref[0], 1.0, 0.0
    )

    def turn(degrees):
        def rows(i, _):
            start = pl.multiple_of(i * 16, 16)
            for n in range(EDGES // 128):
                lanes = slice(n * 128, (n + 1) * 128)
                cols = [picked[pl.ds(b * CH + start, 16), lanes] for b in range(L0)]
                for a in degrees:
                    acc = None
                    for b in range(L0):
                        row = (a * L0 + b) * (EDGES // 128) + n
                        term = rot_ref[a * L0 + b, n : n + 1, :] * cols[b]
                        acc = term if acc is None else acc + term
                    rot_t[pl.ds(a * CH + start, 16), lanes] = (acc * live[:, lanes]).astype(BF16)
            return 0

        lax.fori_loop(0, CH // 16, rows, 0)

    load[1].wait()
    turn((0, 1))

    pl.semaphore_wait(barrier, len(greeted))

    own_lanes = pl.ds(pl.multiple_of(lax.rem(y, LANES) * 128, 128), 128)
    w_copy = send(
        w_hbm.at[:, :, own_lanes], wo, w_send.at[0], w_recv.at[0], at(g, y, mirror)
    )

    @pl.when(y < LANES)
    def _():
        w_copy.start()

    load[2].wait()
    for h in range(GROUP):
        block = None
        for half in range(2):
            first = half * (K // 2) + h * ROWS
            lo = first // 128 * 128
            hi = -(-(first + ROWS) // 128) * 128
            put = onehot(
                (hi - lo, 128),
                lambda r, l, half=half, d=first - lo: (r == d + l - half * 64)
                & (l >= half * 64) & (l < half * 64 + ROWS),
            )
            part_of = dot(in_ref[:, lo:hi], put)
            block = part_of if block is None else block + part_of
        in_pad[:, h * 128 : (h + 1) * 128] = block.astype(BF16)

    def g_copies(q, other):
        out = []
        for k in range(GROUP):
            g_to = lax.rem(g + k, GROUP)
            if k > 0:
                out.append(send(
                    gs.at[q, py, g_to], gr.at[q, g], g_send.at[q, k], g_recv.at[q, k], at(g_to, y, z)
                ))
            out.append(send(
                gs.at[q, 1 - py, g_to], gr.at[q, GROUP + g],
                g_send.at[q, GROUP + k], g_recv.at[q, GROUP + k], at(g_to, other, z),
            ))
        return out

    def g_own(q):
        return pltpu.make_async_copy(gs.at[q, py, g], gr.at[q, g], g_self.at[q])

    def grad_chunk(q, other):
        for p in range(2):
            rows = rot_t[(2 * q + p) * 112 : (2 * q + p + 1) * 112, :]
            for h in range(0, GROUP, 2):
                block = dot(rows, in_pad[:, h * 128 : (h + 2) * 128]).astype(BF16)
                gs[q, p, h] = block[:, :128]
                gs[q, p, h + 1] = block[:, 128:]
        g_own(q).start()
        for copy in g_copies(q, other):
            copy.start()

    others = [near, near, far, far]
    for q in range(QS):
        if q > 0:
            turn(((2, 3), (4, 5), (6,))[q - 1])
        grad_chunk(q, others[q])
    rot_n[...] = rot_t[...].T

    spread = onehot((256, 16), lambda m, e: m % 16 == e)
    gather = onehot((16, 256), lambda s, k: k // 16 == s)
    same = onehot((256, 256), lambda m, k: m // 16 == k % 16).astype(F32)
    for pair in range(2):
        coef = ct_ref[pair]
        high = coef.astype(BF16)
        low = (coef - high.astype(F32)).astype(BF16)
        for n, piece in enumerate((high, low)):
            wide = dot(dot(spread, piece).astype(BF16), gather)
            mix[pair, n] = (wide * same).astype(BF16)

    low_lanes = lax.broadcasted_iota(jnp.int32, (16, 128), 1) < 64

    def swap(v):
        return pltpu.roll(v, 64, 1)

    def contract(q):
        g_own(q).wait()
        for copy in g_copies(q, others[q]):
            copy.wait_recv()
        for t in range(7):
            block = gr[q, :, t * 16 : (t + 1) * 16, :].reshape(256, 128)
            made = dot(mix[q // 2, 0], block) + dot(mix[q // 2, 1], block)
            area[t * 16 : (t + 1) * 16] = made.reshape(16, 16, 128)

        def pack(i, _):
            for k in range(HALF):
                first, second = area[i * COLS + k], area[i * COLS + HALF + k]
                part[q, i, k] = jnp.where(low_lanes, first, swap(second))
                part[q, NZL + i, k] = jnp.where(low_lanes, swap(first), second)
            return 0

        lax.fori_loop(0, NZL, pack, 0)

    def steps(q, way):
        return 8 if way == q % 2 else 7

    def z_copy(q, way, s):
        return send(
            zs.at[q, way, s], zr.at[q, way, s], z_send.at[q, way, s], z_recv.at[q, way, s],
            at(g, y, up if way == 0 else down),
        )

    def ring_step(q, s):
        for way in range(2):
            n = steps(q, way)
            if s >= n:
                continue
            ahead = n - s
            owner = lax.rem(z + ahead, NZ) if way == 0 else lax.rem(z + NZ - ahead, NZ)
            value = part[q, owner]
            if s > 0:
                z_copy(q, way, s - 1).wait_recv()
                value += zr[q, way, s - 1].astype(F32)
            zs[q, way, s] = value.astype(BF16)
            z_copy(q, way, s).start()

    def ring_end(q):
        value = part[q, z]
        for way in range(2):
            n = steps(q, way)
            z_copy(q, way, n - 1).wait_recv()
            value += zr[q, way, n - 1].astype(F32)
        total[q] = value

    def m_copies():
        return [
            send(
                ms.at[lax.rem(g + k, GROUP)], mr.at[zh * GROUP + g], m_send.at[k], m_recv.at[k],
                at(lax.rem(g + k, GROUP), y, z),
            )
            for k in range(1, GROUP)
        ]

    def m_own():
        return pltpu.make_async_copy(ms.at[g], mr.at[zh * GROUP + g], m_self.at[0])

    tail = jnp.zeros((8, 128), F32)

    def mixed(first, source, lanes):
        sums = [None] * 4
        for e in range(0, EXPERTS, 2):
            both = source[e // 2, :, lanes].astype(F32)
            for j in range(4):
                term = coef_ref[first + j, e] * both[:ROWS] + coef_ref[first + j, e + 1] * both[ROWS:]
                sums[j] = term if e == 0 else sums[j] + term
        return [jnp.concatenate([v, tail], 0).astype(BF16) for v in sums]

    def merge_own():
        def block(i, _):
            lanes = pl.ds(pl.multiple_of(i * 128, 128), 128)
            for first in range(0, GROUP, 4):
                for j, v in enumerate(mixed(y * GROUP + first, w_ref, lanes)):
                    ms[first + j, i] = v
            return 0

        load[3].wait()
        lax.fori_loop(0, LANES, block, 0)
        m_own().start()
        for copy in m_copies():
            copy.start()

    def o_copies(n):
        return [
            send(
                mo.at[n, lax.rem(g + k, GROUP)], mr.at[(1 - zh) * GROUP + g, lax.rem(y, LANES)],
                o_send.at[n, k], o_recv.at[n, k], at(lax.rem(g + k, GROUP), lax.rem(y + n, NY), z),
            )
            for k in range(GROUP) if n + k > 0
        ]

    def o_own():
        return pltpu.make_async_copy(
            mo.at[0, g], mr.at[(1 - zh) * GROUP + g, lax.rem(y, LANES)], m_self.at[1]
        )

    def merge_other(n):
        @pl.when(y < LANES)
        def _():
            if n == FIRST_N:
                w_copy.wait_recv()
            for first in range(0, GROUP, 4):
                rows = lax.rem(y + n, NY) * GROUP + first
                for j, v in enumerate(mixed(rows, wo, slice(None))):
                    mo[n, first + j] = v
            if n == 0:
                o_own().start()
            for copy in o_copies(n):
                copy.start()

    def other_came(n):
        @pl.when(lax.rem(y + NY - n, NY) < LANES)
        def _():
            if n == 0:
                o_own().wait()
            for copy in o_copies(n):
                copy.wait_recv()

    def other_left(n):
        @pl.when(y < LANES)
        def _():
            for copy in o_copies(n):
                copy.wait_send()

    done = [0] * QS

    def advance(q, count=1):
        for _ in range(count):
            if done[q] < 8:
                ring_step(q, done[q])
                done[q] += 1

    for q in range(QS):
        if q == OWN_AT:
            merge_own()
        contract(q)
        advance(q)
        if q == 2:
            advance(0)
    for wave in range(7):
        if wave + QS == OWN_AT:
            merge_own()
        for n in OTHER_AT[wave]:
            merge_other(n)
        for q in range(QS):
            advance(q)
    for q in range(QS):
        ring_end(q)

    def y_copy(k):
        q = lax.rem(yq + k, QS)
        return send(ys.at[k], yr.at[k], y_send.at[k], y_recv.at[k], at(g, 2 * q + py, z))

    for k in range(1, QS):
        ys[k] = total[lax.rem(yq + k, QS)].astype(BF16)
        y_copy(k).start()

    m_own().wait()
    for copy in m_copies():
        copy.wait_recv()
    for n in range(NY):
        other_came(n)
    for i in range(LANES):
        blocks = [mr[f, i].astype(F32)[:ROWS] for f in range(2 * GROUP)]
        mg[:, i * 128 : (i + 1) * 128] = jnp.concatenate(blocks, 0).astype(BF16)
    for lo in range(0, EDGES, 128):
        eg_ref[lo : lo + 128, :] = lax.dot_general(
            rot_n[lo : lo + 128, :], mg[...], (((1,), (1,)), ((), ())), preferred_element_type=F32
        ).astype(BF16)

    value = total[yq]
    for k in range(1, QS):
        y_copy(k).wait_recv()
        value += yr[k].astype(F32)
    for k in range(HALF):
        xg_ref[k] = value[k]
        xg_ref[HALF + k] = swap(value[k])


    @pl.when(y < LANES)
    def _():
        w_copy.wait_send()

    for q in range(QS):
        for copy in g_copies(q, others[q]):
            copy.wait_send()
        for way in range(2):
            for s in range(steps(q, way)):
                z_copy(q, way, s).wait_send()
    for k in range(1, QS):
        y_copy(k).wait_send()
    for copy in m_copies():
        copy.wait_send()
    for n in range(NY):
        other_left(n)


def per_device(
    expert_weights, coefficients, edge_inputs, node_cotangent, rotations, targets, counts
):
    dp, fs = lax.axis_index("dp"), lax.axis_index("fsdp")
    y, zl, zh = lax.div(dp, NZL), lax.rem(dp, NZL), lax.div(fs, GROUP)

    grouped = coefficients.reshape(NY, NZL, 2, GROUP, EXPERTS)
    level = lax.dynamic_slice(grouped, (0, zl, zh, 0, 0), (NY, 1, 1, GROUP, EXPERTS))
    level = level.reshape(NY, GROUP, EXPERTS)

    def of_group(y_of):
        return lax.dynamic_slice_in_dim(level, y_of, 1, 0)[0]

    py = lax.rem(y, 2)
    own = of_group(y)
    pairs = jnp.stack([
        jnp.concatenate([own, of_group(y + 1 - 2 * py)], 0).T,
        jnp.concatenate([own, of_group(lax.rem(y + 7 + 2 * py, NY))], 0).T,
    ])
    vmem, smem = pl.BlockSpec(memory_space=pltpu.VMEM), pl.BlockSpec(memory_space=pltpu.SMEM)
    hbm = pl.BlockSpec(memory_space=pltpu.HBM)
    dma, shape = pltpu.SemaphoreType.DMA, pltpu.VMEM
    edge_grads, grads = pl.pallas_call(
        kernel,
        out_shape=(
            jax.ShapeDtypeStruct((EDGES, K), BF16),
            jax.ShapeDtypeStruct((COLS, EXPERTS, 128), F32),
        ),
        in_specs=[hbm, smem, vmem, hbm, hbm, hbm, vmem, smem],
        out_specs=(vmem, vmem),
        scratch_shapes=[
            shape((NY, 112, K), BF16),
            shape((EDGES, K), BF16),
            shape((ATOMS, K), BF16),
            shape((L0 * L0, EDGES // 128, 128), F32),
            dma((4,)),
            shape((K, EDGES), F32),
            shape((K, EDGES), BF16),
            shape((EDGES, K), BF16),
            shape((EDGES, GROUP * 128), BF16),
            shape((2, 2, 256, 256), BF16),
            shape((QS, 2, GROUP, 112, 128), BF16),
            shape((QS, 2 * GROUP, 112, 128), BF16),
            shape((112, EXPERTS, 128), F32),
            shape((QS, NZ, HALF, EXPERTS, 128), F32),
            shape((QS, 2, 8, HALF, EXPERTS, 128), BF16),
            shape((QS, 2, 8, HALF, EXPERTS, 128), BF16),
            shape((QS, HALF, EXPERTS, 128), F32),
            shape((QS, HALF, EXPERTS, 128), BF16),
            shape((QS, HALF, EXPERTS, 128), BF16),
            shape((NY, 112, 128), BF16),
            shape((GROUP, LANES, 64, 128), BF16),
            shape((NY, GROUP, 64, 128), BF16),
            shape((2 * GROUP, LANES, 64, 128), BF16),
            shape((K, K), BF16),
            dma((QS, 16)), dma((QS, 16)), dma((QS,)),
            dma((QS, 2, 8)), dma((QS, 2, 8)),
            dma((QS,)), dma((QS,)),
            dma((1,)), dma((1,)),
            dma((NY, GROUP)), dma((NY, GROUP)),
            dma((GROUP,)), dma((GROUP,)), dma((2,)),
        ],
        compiler_params=pltpu.CompilerParams(
            collective_id=0, has_side_effects=True, vmem_limit_bytes=60 * 1024 * 1024
        ),
        name="edge_block_backward",
    )(
        expert_weights.reshape(NY, 112, K),
        level.reshape(NY * GROUP, EXPERTS),
        pairs,
        edge_inputs[0],
        node_cotangent[0],
        rotations.reshape(L0 * L0, EDGES // 128, 128),
        targets,
        counts,
    )
    return edge_grads[None], jnp.transpose(grads[:, :, :ROWS], (1, 2, 0))


def solution(mesh):
    placed = (
        P(None, "fsdp", None),
        P(),
        P(("dp", "fsdp"), None, None),
        P(("dp", "fsdp"), None, None),
        P(("dp", "fsdp"), None, None, None),
        P(("dp", "fsdp"), None),
        P(("dp", "fsdp")),
    )
    return jax.shard_map(
        per_device,
        mesh=mesh,
        in_specs=placed,
        out_specs=(P(("dp", "fsdp"), None, None), P(None, "fsdp", "dp")),
        check_vma=False,
    )
```
